32 devices in a mesh: slab: 8 (over z, x), chan: 4 (over y, core).
Axes of the slice: x: 2, y: 2, z: 4, core: 2. Of those that a mesh axis runs over, the one named last changes fastest.
Arguments:
- volume: bfloat16 [64, 8, 16, 128], P('chan', 'slab'), may hold values from -6 to 6
- kernel: bfloat16 [3, 3, 3, 64, 128], P(None, None, None, None, 'chan'), may hold values from -0.15625 to 0.15625
- bias: float32 [128], P('chan'), may hold values from -3 to 3
- out_grad: bfloat16 [128, 8, 16, 128], P('chan', 'slab'), may hold values from -6 to 6
Outputs:
- feature: bfloat16 [128, 8, 16, 128], P('chan', 'slab')
- input_grad: bfloat16 [64, 8, 16, 128], P('chan', 'slab')
- kernel_grad: float32 [3, 3, 3, 64, 128], P(None, None, None, None, 'chan')
- bias_grad: float32 [128], P('chan')
The draws below stay inside these ranges and needn't reach their ends.
All inputs are finite; a program needn't handle non-finite values.
Results may differ from the reference program's by a relative error of at most 0.00105.
Values may be sent and summed in bfloat16 or wider, within the bound.
A program may use at most 64 MiB of HBM per device.

```python
import jax
import jax.numpy as jnp
from jax import lax

CIN = 64
COUT = 128
ROWS = 16
COLS = 128
DEPTH = 8


def steps_of(key, extent, cuts, low, top_value):
    def one(position, blocks):
        steps = jax.random.uniform(jax.random.fold_in(jax.random.fold_in(key, 6), position), (blocks,), jnp.float32, low / len(cuts), top_value / len(cuts))
        return jnp.repeat(jnp.exp(steps), extent[position] // blocks).reshape((-1,) + (1,) * (len(extent) - position - 1))

    level = one(*cuts[0])
    for cut in cuts[1:]:
        level = level * one(*cut)
    return level


def bell_draw(rng, shape, scale, reach, pieces=(), held_as=jnp.bfloat16):
    result = jax.random.normal(rng, shape, jnp.float32) * scale
    if len(pieces) > 0:
        result = steps_of(rng, shape, pieces, -0.22, 0.18) * result
    return jnp.clip(result, min=-reach, max=reach).astype(held_as)


def setup_inputs(seed: int = 0) -> dict:
    key_list = jax.random.split(jax.random.key(seed), 5)
    volume = bell_draw(key_list[0], (CIN, DEPTH, ROWS, COLS), 1.0, 6.0, ((0, 4), (1, 8)))
    kernel = bell_draw(key_list[1], (3, 3, 3, CIN, COUT), (27 * CIN) ** -0.5, 0.15625, ((4, 4),))
    bias = bell_draw(key_list[2], (COUT,), 0.5, 3.0, ((0, 4),), jnp.float32)
    out_grad = bell_draw(key_list[3], (COUT, DEPTH, ROWS, COLS), 1.0, 6.0, ((0, 4), (1, 8)))
    return {"volume": volume, "kernel": kernel, "bias": bias, "out_grad": out_grad}


def convolve(volume_f, kernel_f):
    return lax.conv_general_dilated(volume_f[None], kernel_f, (1, 1, 1), ((1, 1), (1, 1), (1, 1)), dimension_numbers=('NCDHW', 'DHWIO', 'NCDHW'), precision=lax.Precision.HIGHEST)[0]

def reference(volume, kernel, bias, out_grad):
    volume_f = volume.astype(jnp.float32)
    kernel_f = kernel.astype(jnp.float32)
    pre, pullback = jax.vjp(convolve, volume_f, kernel_f)
    feature = (pre + bias[:, None, None, None]).astype(jnp.bfloat16)
    grad_f = out_grad.astype(jnp.float32)
    volume_grad, weight_grad = pullback(grad_f)
    factor = 1.0 / jnp.sqrt(jnp.float32(DEPTH * ROWS * COLS))
    bias_grad = lax.optimization_barrier(jnp.sum(grad_f, axis=(1, 2, 3))) * factor
    return (feature, volume_grad.astype(jnp.bfloat16), weight_grad * factor, bias_grad)
```

```python
import functools
import math

import jax
import jax.numpy as jnp
from jax import lax
from jax.experimental import pallas as pl
from jax.experimental.pallas import tpu as pltpu
from jax.sharding import PartitionSpec as P

F32 = jnp.float32
BF16 = jnp.bfloat16
MESH = pl.DeviceIdType.MESH


def roll_cols(value, step):
    width = value.shape[-1]
    lane = lax.broadcasted_iota(jnp.int32, value.shape, value.ndim - 1)
    edge = 0 if step > 0 else width - 1
    return jnp.where(lane == edge, 0.0, pltpu.roll(value, step % width, value.ndim - 1))


def body(slabs, chans, packed, scale, vol, ker, bias, og, feat, ig, kg, bg,
         tmp, rv, rg, xv3, xg3, vc, w1, w2, igs, igr, part, rs_s, rs_r, ag_r,
         v_send, v_recv, vh_send, g_send, g_recv, ig_send, ig_recv,
         rs_send, rs_recv, ag_send, ag_recv):
    c_in, o_loc = ker.shape[3], ker.shape[4]
    c_loc, rows, cols = vol.shape[0], vol.shape[2], vol.shape[3]
    cells = rows * cols
    s = lax.axis_index("slab")
    c = lax.axis_index("chan")
    has_prev, has_next = s > 0, s < slabs - 1

    def to_slab(t):
        return {"slab": t}

    def to_chan(t):
        return {"chan": t}

    peers = [lax.rem(c + k, chans) for k in range(1, chans)]
    others = [lax.rem(s + k, slabs) for k in range(1, slabs)] if packed else []

    barrier = pltpu.get_barrier_semaphore()
    for p in peers:
        pl.semaphore_signal(barrier, inc=1, device_id=to_chan(p), device_id_type=MESH)
    if packed:
        for t in others:
            pl.semaphore_signal(barrier, inc=1, device_id=to_slab(t), device_id_type=MESH)
    else:
        @pl.when(has_prev)
        def _():
            pl.semaphore_signal(barrier, inc=1, device_id=to_slab(s - 1), device_id_type=MESH)

        @pl.when(has_next)
        def _():
            pl.semaphore_signal(barrier, inc=1, device_id=to_slab(s + 1), device_id_type=MESH)

    tmp[...] = og[:, 0].astype(F32)
    for h in range(rows):
        rg[1, :, h * cols:(h + 1) * cols] = tmp[:, h, :].astype(BF16)
    tmp[:c_loc] = vol[:, 0].astype(F32)
    for h in range(rows):
        rv[1, c, :, h * cols:(h + 1) * cols] = tmp[:c_loc, h, :].astype(BF16)

    if packed:
        pl.semaphore_wait(barrier, chans - 1 + slabs - 1)
    else:
        pl.semaphore_wait(barrier, chans - 1)

        @pl.when(has_prev)
        def _():
            pl.semaphore_wait(barrier, 1)

        @pl.when(has_next)
        def _():
            pl.semaphore_wait(barrier, 1)

    def copy(src, dst, ssem, rsem, dev):
        return pltpu.make_async_remote_copy(
            src_ref=src, dst_ref=dst, send_sem=ssem, recv_sem=rsem,
            device_id=dev, device_id_type=MESH)

    g_up = copy(rg.at[1], rg.at[2], g_send.at[0], g_recv.at[2], to_slab(s + 1))
    g_down = copy(rg.at[1], rg.at[0], g_send.at[1], g_recv.at[0], to_slab(s - 1))
    v_up = copy(rv.at[1, c], rv.at[0, c], vh_send.at[0], v_recv.at[0, c], to_slab(s + 1))
    v_down = copy(rv.at[1, c], rv.at[2, c], vh_send.at[1], v_recv.at[2, c], to_slab(s - 1))

    def v_chan(a, p):
        return copy(rv.at[a, c], rv.at[a, c], v_send.at[a, p], v_recv.at[a, c], to_chan(p))

    def v_from(a, q):
        return copy(rv.at[a, q], rv.at[a, q], v_send.at[a, q], v_recv.at[a, q], to_chan(q))

    own_v = [v_chan(1, p) for p in peers]
    for d in own_v:
        d.start()

    @pl.when(has_next)
    def _():
        g_up.start()
        v_up.start()

    @pl.when(has_prev)
    def _():
        g_down.start()
        v_down.start()

    for cc in range(3):
        w2[cc * c_in:(cc + 1) * c_in, :] = jnp.concatenate(
            [ker[a, 2 - j, cc].astype(F32) for j in range(3) for a in range(3)], axis=1
        ).astype(BF16)
    wt = jnp.concatenate(
        [jnp.concatenate([ker[a, b, cc].astype(F32) for cc in range(3)], axis=1)
         for b in range(3) for a in range(3)], axis=0)
    w1[...] = jnp.transpose(wt).astype(BF16)

    def windows(dst, a, block):
        n = block.shape[0]
        zero = jnp.zeros((n, cols), BF16)
        for j in range(3):
            at = j * 3 * n + a * n
            if j == 1:
                dst[at:at + n, :] = block
            elif j == 0:
                dst[at:at + n, 0:cols] = zero
                dst[at:at + n, cols:cells] = block[:, 0:cells - cols]
            else:
                dst[at:at + n, 0:cells - cols] = block[:, cols:cells]
                dst[at:at + n, cells - cols:cells] = zero

    windows(xg3, 1, rg[1])
    vc[3 * c_in:, :] = jnp.ones((16, cells), BF16)

    for q in peers:
        v_from(1, q).wait_recv()
    v_own = jnp.concatenate([rv[1, q] for q in range(chans)], axis=0)
    windows(xv3, 1, v_own)
    for h in range(rows):
        block = v_own[:, h * cols:(h + 1) * cols]
        wide = block.astype(F32)
        at = slice(h * cols, (h + 1) * cols)
        vc[0:c_in, at] = roll_cols(wide, 1).astype(BF16)
        vc[c_in:2 * c_in, at] = block
        vc[2 * c_in:3 * c_in, at] = roll_cols(wide, -1).astype(BF16)

    @pl.when(has_next)
    def _():
        g_down.wait_recv()

    @pl.when(jnp.logical_not(has_next))
    def _():
        rg[0] = jnp.zeros((o_loc, cells), BF16)

    windows(xg3, 0, rg[0])

    @pl.when(has_prev)
    def _():
        g_up.wait_recv()

    @pl.when(jnp.logical_not(has_prev))
    def _():
        rg[2] = jnp.zeros((o_loc, cells), BF16)

    windows(xg3, 2, rg[2])

    part[:, 0:9 * o_loc] = lax.dot_general(
        vc[...], xg3[...], (((1,), (1,)), ((), ())), preferred_element_type=F32)
    if packed:
        ones_sum = part[3 * c_in:3 * c_in + 8, 4 * o_loc:5 * o_loc]
        for t in range(slabs):
            for r in range(3):
                at = 24 * t + 8 * r
                rs_s[t, 2 * r] = part[at:at + 8, 0:128]
                rs_s[t, 2 * r + 1] = part[at:at + 8, 128:256]
            rs_s[t, 6] = jnp.concatenate(
                [part[24 * t + 8 * r:24 * t + 8 * r + 8, 256:288] for r in range(3)]
                + [ones_sum], axis=1)
        rs_out = [copy(rs_s.at[t], rs_r.at[s], rs_send.at[t], rs_recv.at[s], to_slab(t))
                  for t in others]
        for d in rs_out:
            d.start()

    @pl.when(has_prev)
    def _():
        v_up.wait_recv()
        for p in peers:
            v_chan(0, p).start()

    @pl.when(has_next)
    def _():
        v_down.wait_recv()
        for p in peers:
            v_chan(2, p).start()

    share = jnp.dot(w2[...], xg3[...], preferred_element_type=F32)
    for h in range(rows):
        at = slice(h * cols, (h + 1) * cols)
        total = (share[c_in:2 * c_in, at] + roll_cols(share[0:c_in, at], -1)
                 + roll_cols(share[2 * c_in:3 * c_in, at], 1))
        for p in range(chans):
            igs[p, :, at] = total[p * c_loc:(p + 1) * c_loc]
    ig_out = [copy(igs.at[p], igr.at[c], ig_send.at[p], ig_recv.at[c], to_chan(p)) for p in peers]
    for d in ig_out:
        d.start()

    if packed:
        rs_r[s] = rs_s[s]
        for t in others:
            copy(rs_s.at[t], rs_r.at[t], rs_send.at[t], rs_recv.at[t], to_slab(t)).wait_recv()
        done = rs_r[0]
        for t in range(1, slabs):
            done = done + rs_r[t]
        done = done * scale
        ag_r[s] = done
        bg[...] = done[6, 0:1, 3 * o_loc:4 * o_loc]
        ag_out = [copy(ag_r.at[s], ag_r.at[s], ag_send.at[t], ag_recv.at[s], to_slab(t))
                  for t in others]
        for d in ag_out:
            d.start()
    else:
        bg[...] = part[3 * c_in:3 * c_in + 1, 4 * o_loc:5 * o_loc]
        for cc in range(3):
            for a in range(3):
                for b in range(3):
                    m = (2 - b) * 3 + a
                    kg[a, b, cc] = part[cc * c_in:(cc + 1) * c_in, m * o_loc:(m + 1) * o_loc]

    for a, here in ((0, has_prev), (2, has_next)):
        @pl.when(here)
        def _():
            for q in peers:
                v_from(a, q).wait_recv()

        @pl.when(jnp.logical_not(here))
        def _():
            rv[a] = jnp.zeros((chans, c_loc, cells), BF16)

        windows(xv3, a, jnp.concatenate([rv[a, q] for q in range(chans)], axis=0))
    pre = jnp.dot(w1[...], xv3[...], preferred_element_type=F32)
    bias_col = jnp.transpose(jnp.broadcast_to(bias[...], (cols, o_loc)))
    for h in range(rows):
        at = slice(h * cols, (h + 1) * cols)
        tmp[:, h, :] = (pre[o_loc:2 * o_loc, at] + roll_cols(pre[0:o_loc, at], 1)
                        + roll_cols(pre[2 * o_loc:3 * o_loc, at], -1) + bias_col)
    feat[:, 0] = tmp[...].astype(BF16)

    igr[c] = igs[c]
    for q in peers:
        copy(igs.at[q], igr.at[q], ig_send.at[q], ig_recv.at[q], to_chan(q)).wait_recv()
    for h in range(rows):
        at = slice(h * cols, (h + 1) * cols)
        total = igr[0, :, at]
        for q in range(1, chans):
            total = total + igr[q, :, at]
        tmp[:c_loc, h, :] = total
    ig[:, 0] = tmp[:c_loc].astype(BF16)

    if packed:
        for t in others:
            copy(ag_r.at[t], ag_r.at[t], ag_send.at[t], ag_recv.at[t], to_slab(t)).wait_recv()
        for t in range(slabs):
            for r in range(3):
                row = 24 * t + 8 * r
                cc, i = row // c_in, row % c_in
                for a in range(3):
                    for b in range(3):
                        m = (2 - b) * 3 + a
                        if m < 8:
                            k, lane = 2 * r + m // 4, (m % 4) * 32
                        else:
                            k, lane = 6, 32 * r
                        kg[a, b, cc, i:i + 8, :] = ag_r[t, k, :, lane:lane + 32]

    for d in own_v:
        d.wait_send()

    @pl.when(has_next)
    def _():
        g_up.wait_send()
        v_up.wait_send()
        for p in peers:
            v_chan(2, p).wait_send()

    @pl.when(has_prev)
    def _():
        g_down.wait_send()
        v_down.wait_send()
        for p in peers:
            v_chan(0, p).wait_send()

    for d in ig_out:
        d.wait_send()
    if packed:
        for d in rs_out + ag_out:
            d.wait_send()


def on_device(slabs, chans, volume, kernel, bias, out_grad):
    c_loc, _, rows, cols = volume.shape
    c_in, o_loc = kernel.shape[3], kernel.shape[4]
    cells = rows * cols
    packed = o_loc == 32 and 3 * c_in == 24 * slabs
    scale = 1.0 / math.sqrt(slabs * cells)
    vmem = pl.BlockSpec(memory_space=pltpu.VMEM)
    lanes = -(-9 * o_loc // 128) * 128
    parts = slabs if packed else 1
    dma = pltpu.SemaphoreType.DMA
    feature, input_grad, kernel_grad, bias_grad = pl.pallas_call(
        functools.partial(body, slabs, chans, packed, scale),
        out_shape=(
            jax.ShapeDtypeStruct((o_loc, 1, rows, cols), BF16),
            jax.ShapeDtypeStruct((c_loc, 1, rows, cols), BF16),
            jax.ShapeDtypeStruct(kernel.shape, F32),
            jax.ShapeDtypeStruct((1, o_loc), F32),
        ),
        in_specs=[vmem] * 4,
        out_specs=(vmem,) * 4,
        scratch_shapes=[
            pltpu.VMEM((max(o_loc, c_loc), rows, cols), F32),
            pltpu.VMEM((3, chans, c_loc, cells), BF16),
            pltpu.VMEM((3, o_loc, cells), BF16),
            pltpu.VMEM((9 * c_in, cells), BF16),
            pltpu.VMEM((9 * o_loc, cells), BF16),
            pltpu.VMEM((3 * c_in + 16, cells), BF16),
            pltpu.VMEM((3 * o_loc, 9 * c_in), BF16),
            pltpu.VMEM((3 * c_in, 9 * o_loc), BF16),
            pltpu.VMEM((chans, c_loc, cells), F32),
            pltpu.VMEM((chans, c_loc, cells), F32),
            pltpu.VMEM((3 * c_in + 16, lanes), F32),
            pltpu.VMEM((parts, 7, 8, 128), F32),
            pltpu.VMEM((parts, 7, 8, 128), F32),
            pltpu.VMEM((parts, 7, 8, 128), F32),
            dma((3, chans)), dma((3, chans)), dma((2,)), dma((2,)), dma((3,)),
            dma((chans,)), dma((chans,)),
            dma((parts,)), dma((parts,)), dma((parts,)), dma((parts,)),
        ],
        compiler_params=pltpu.CompilerParams(
            collective_id=0, has_side_effects=True, vmem_limit_bytes=40 * 1024 * 1024),
        cost_estimate=pl.CostEstimate(
            flops=3 * 2 * cells * 27 * c_in * o_loc, bytes_accessed=2 * 1024 * 1024,
            transcendentals=0),
    )(volume, kernel, bias.reshape(1, o_loc), out_grad)
    bias_grad = bias_grad.reshape(o_loc)
    if not packed:
        kernel_grad, bias_grad = lax.psum((kernel_grad, bias_grad), "slab")
        kernel_grad, bias_grad = kernel_grad * scale, bias_grad * scale
    return feature, input_grad, kernel_grad, bias_grad


def solution(mesh):
    specs = (
        P("chan", "slab", None, None),
        P(None, None, None, None, "chan"),
        P("chan"),
        P("chan", "slab", None, None),
    )
    out_specs = (specs[0], specs[0], specs[1], specs[2])
    run = functools.partial(on_device, mesh.shape["slab"], mesh.shape["chan"])
    return jax.shard_map(run, mesh=mesh, in_specs=specs, out_specs=out_specs, check_vma=False)
```

```python
import functools
import math

import jax
import jax.numpy as jnp
from jax import lax
from jax.experimental import pallas as pl
from jax.experimental.pallas import tpu as pltpu
from jax.sharding import PartitionSpec as P

F32 = jnp.float32
BF16 = jnp.bfloat16
MESH = pl.DeviceIdType.MESH


def roll_cols(value, step):
    width = value.shape[-1]
    lane = lax.broadcasted_iota(jnp.int32, value.shape, value.ndim - 1)
    edge = 0 if step > 0 else width - 1
    return jnp.where(lane == edge, 0.0, pltpu.roll(value, step % width, value.ndim - 1))


def body(slabs, chans, packed, scale, vol, ker, bias, og, feat, ig, kg, bg,
         tmp, rv, rg, xv3, xg3, vc, w1, w2, igs, igr, part,
         s1, r1, a1, s2, r2, a2,
         v_send, v_recv, vh_send, g_send, g_recv, ig_send, ig_recv,
         s1_send, s1_recv, a1_send, a1_recv, s2_send, s2_recv, a2_send, a2_recv):
    o_loc, c_in = ker.shape[3], ker.shape[4]
    c_loc, rows, cols = vol.shape[0], vol.shape[2], vol.shape[3]
    cells = rows * cols
    s = lax.axis_index("slab")
    c = lax.axis_index("chan")
    has_prev, has_next = s > 0, s < slabs - 1

    def to_slab(t):
        return {"slab": t}

    def to_chan(t):
        return {"chan": t}

    def other_core(q):
        return q + 1 - 2 * lax.rem(q, 2)

    peers = [lax.rem(c + k, chans) for k in range(1, chans)]
    sib = other_core(c)
    same = [lax.rem(c + 2 * k, chans) for k in range(1, chans // 2)]
    others = [lax.rem(s + k, slabs) for k in range(1, slabs)] if packed else []

    barrier = pltpu.get_barrier_semaphore()
    for p in peers:
        pl.semaphore_signal(barrier, inc=1, device_id=to_chan(p), device_id_type=MESH)
    if packed:
        for t in others:
            pl.semaphore_signal(barrier, inc=1, device_id=to_slab(t), device_id_type=MESH)
    else:
        @pl.when(has_prev)
        def _():
            pl.semaphore_signal(barrier, inc=1, device_id=to_slab(s - 1), device_id_type=MESH)

        @pl.when(has_next)
        def _():
            pl.semaphore_signal(barrier, inc=1, device_id=to_slab(s + 1), device_id_type=MESH)

    tmp[...] = og[:, 0].astype(F32)
    for h in range(rows):
        rg[1, :, h * cols:(h + 1) * cols] = tmp[:, h, :].astype(BF16)
    tmp[:c_loc] = vol[:, 0].astype(F32)
    for h in range(rows):
        rv[1, c, :, h * cols:(h + 1) * cols] = tmp[:c_loc, h, :].astype(BF16)

    if packed:
        pl.semaphore_wait(barrier, chans - 1 + slabs - 1)
    else:
        pl.semaphore_wait(barrier, chans - 1)

        @pl.when(has_prev)
        def _():
            pl.semaphore_wait(barrier, 1)

        @pl.when(has_next)
        def _():
            pl.semaphore_wait(barrier, 1)

    def copy(src, dst, ssem, rsem, dev):
        return pltpu.make_async_remote_copy(
            src_ref=src, dst_ref=dst, send_sem=ssem, recv_sem=rsem,
            device_id=dev, device_id_type=MESH)

    g_up = copy(rg.at[1], rg.at[2], g_send.at[0], g_recv.at[2], to_slab(s + 1))
    g_down = copy(rg.at[1], rg.at[0], g_send.at[1], g_recv.at[0], to_slab(s - 1))
    v_up = copy(rv.at[1, c], rv.at[0, c], vh_send.at[0], v_recv.at[0, c], to_slab(s + 1))
    v_down = copy(rv.at[1, c], rv.at[2, c], vh_send.at[1], v_recv.at[2, c], to_slab(s - 1))

    def v_block(a, q, p, slot):
        return copy(rv.at[a, q], rv.at[a, q], v_send.at[a, slot], v_recv.at[a, q], to_chan(p))

    def v_first(a):
        return [v_block(a, c, p, p) for p in same] + [v_block(a, c, sib, sib)]

    def v_relay(a):
        return [v_block(a, q, sib, other_core(q)) for q in same]

    def v_relay_wait(a):
        for q, d in zip(same, v_relay(a)):
            v_block(a, q, sib, other_core(q)).wait_recv()
            d.start()

    def v_rest_wait(a):
        for q in [sib] + [other_core(q) for q in same]:
            v_block(a, q, sib, q).wait_recv()

    for d in v_first(1):
        d.start()

    @pl.when(has_next)
    def _():
        g_up.start()

    @pl.when(has_prev)
    def _():
        g_down.start()

    order = (0, 2, 1)
    w2t = jnp.concatenate(
        [jnp.concatenate([ker[a, 2 - j, cc].astype(F32) for cc in range(3)], axis=1)
         for a in order for j in range(3)], axis=0)
    w2[...] = jnp.transpose(w2t).astype(BF16)
    for cc in range(3):
        w1[cc * o_loc:(cc + 1) * o_loc, :] = jnp.concatenate(
            [ker[a, b, cc].astype(F32) for a in range(3) for b in range(3)], axis=1
        ).astype(BF16)

    def windows(dst, base, block):
        n = block.shape[0]
        zero = jnp.zeros((n, cols), BF16)
        at = base * 3 * n
        dst[at:at + n, 0:cols] = zero
        dst[at:at + n, cols:cells] = block[:, 0:cells - cols]
        dst[at + n:at + 2 * n, :] = block
        dst[at + 2 * n:at + 3 * n, 0:cells - cols] = block[:, cols:cells]
        dst[at + 2 * n:at + 3 * n, cells - cols:cells] = zero

    windows(xg3, 2, rg[1])
    nt = (((1,), (1,)), ((), ()))
    bias_part = lax.dot_general(
        jnp.ones((8, cells), BF16), rg[1], nt, preferred_element_type=F32)

    v_relay_wait(1)
    v_rest_wait(1)
    v_own = jnp.concatenate([rv[1, q] for q in range(chans)], axis=0)
    for h in range(rows):
        at = slice(h * cols, (h + 1) * cols)
        block = v_own[:, at]
        wide = block.astype(F32)
        vc[0:c_in, at] = roll_cols(wide, 1).astype(BF16)
        vc[c_in:2 * c_in, at] = block
        vc[2 * c_in:3 * c_in, at] = roll_cols(wide, -1).astype(BF16)

    half = 6 * o_loc
    wide_to = 3 * c_in
    part[half:, 0:wide_to] = lax.dot_general(
        xg3[half:, :], vc[...], nt, preferred_element_type=F32)

    def tiles(start, count):
        found = [part[start + 8 * k:start + 8 * k + 8, 0:128] for k in range(count)]
        for k in range(0, count, 2):
            found.append(jnp.concatenate(
                [part[start + 8 * k:start + 8 * k + 8, 128:192],
                 part[start + 8 * k + 8:start + 8 * k + 16, 128:192]], axis=1))
        return found

    def fill(dst, found):
        per = dst.shape[1]
        found = found + [jnp.zeros((8, 128), F32)] * (per * slabs - len(found))
        for k, tile in enumerate(found):
            dst[k // per, k % per] = tile

    def rs_copy(src, dst, ssem, rsem, t):
        return copy(src.at[t], dst.at[s], ssem.at[t], rsem.at[s], to_slab(t))

    def rs_from(src, dst, ssem, rsem, t):
        return copy(src.at[t], dst.at[t], ssem.at[t], rsem.at[t], to_slab(t))

    def ag_copy(buf, ssem, rsem, t):
        return copy(buf.at[s], buf.at[s], ssem.at[t], rsem.at[s], to_slab(t))

    def ag_from(buf, ssem, rsem, t):
        return copy(buf.at[t], buf.at[t], ssem.at[t], rsem.at[t], to_slab(t))

    def reduce_rows(src, dst, buf, ssem, rsem):
        dst[s] = src[s]
        for t in others:
            rs_from(src, dst, ssem, rsem, t).wait_recv()
        done = dst[0]
        for t in range(1, slabs):
            done = done + dst[t]
        buf[s] = done * scale

    if packed:
        fill(s1, tiles(half, 3 * o_loc // 8)
             + [jnp.concatenate([bias_part, jnp.zeros((8, 128 - o_loc), F32)], axis=1)])
        for t in others:
            rs_copy(s1, r1, s1_send, s1_recv, t).start()

    @pl.when(has_next)
    def _():
        v_up.start()

    @pl.when(has_prev)
    def _():
        v_down.start()

    @pl.when(has_next)
    def _():
        g_down.wait_recv()

    @pl.when(jnp.logical_not(has_next))
    def _():
        rg[0] = jnp.zeros((o_loc, cells), BF16)

    windows(xg3, 0, rg[0])

    @pl.when(has_prev)
    def _():
        g_up.wait_recv()

    @pl.when(jnp.logical_not(has_prev))
    def _():
        rg[2] = jnp.zeros((o_loc, cells), BF16)

    windows(xg3, 1, rg[2])
    part[0:half, 0:wide_to] = lax.dot_general(
        xg3[0:half, :], vc[...], nt, preferred_element_type=F32)
    if packed:
        fill(s2, tiles(0, half // 8))
        for t in others:
            rs_copy(s2, r2, s2_send, s2_recv, t).start()
        reduce_rows(s1, r1, a1, s1_send, s1_recv)
        for t in others:
            ag_copy(a1, a1_send, a1_recv, t).start()

    @pl.when(has_prev)
    def _():
        v_up.wait_recv()
        for d in v_first(0):
            d.start()

    @pl.when(has_next)
    def _():
        v_down.wait_recv()
        for d in v_first(2):
            d.start()

    share = jnp.dot(w2[...], xg3[...], preferred_element_type=F32)
    for h in range(rows):
        at = slice(h * cols, (h + 1) * cols)
        total = (share[c_in:2 * c_in, at] + roll_cols(share[0:c_in, at], -1)
                 + roll_cols(share[2 * c_in:3 * c_in, at], 1))
        for p in range(chans):
            igs[p, :, at] = total[p * c_loc:(p + 1) * c_loc]
    ig_out = [copy(igs.at[p], igr.at[c], ig_send.at[p], ig_recv.at[c], to_chan(p)) for p in peers]
    for d in ig_out:
        d.start()

    @pl.when(has_prev)
    def _():
        v_relay_wait(0)

    @pl.when(has_next)
    def _():
        v_relay_wait(2)

    if packed:
        reduce_rows(s2, r2, a2, s2_send, s2_recv)
        for t in others:
            ag_copy(a2, a2_send, a2_recv, t).start()
    else:
        bg[...] = bias_part[0:1, :]
        for k, a in enumerate(order):
            for j in range(3):
                for cc in range(3):
                    at = (k * 3 + j) * o_loc
                    kg[a, 2 - j, cc] = part[at:at + o_loc, cc * c_in:(cc + 1) * c_in]

    windows(xv3, 1, v_own)
    for a, here in ((0, has_prev), (2, has_next)):
        @pl.when(here)
        def _():
            v_rest_wait(a)

        @pl.when(jnp.logical_not(here))
        def _():
            rv[a] = jnp.zeros((chans, c_loc, cells), BF16)

        windows(xv3, a, jnp.concatenate([rv[a, q] for q in range(chans)], axis=0))
    pre = jnp.dot(w1[...], xv3[...], preferred_element_type=F32)
    bias_col = jnp.transpose(jnp.broadcast_to(bias[...], (cols, o_loc)))
    for h in range(rows):
        at = slice(h * cols, (h + 1) * cols)
        tmp[:, h, :] = (pre[o_loc:2 * o_loc, at] + roll_cols(pre[0:o_loc, at], 1)
                        + roll_cols(pre[2 * o_loc:3 * o_loc, at], -1) + bias_col)
    feat[:, 0] = tmp[...].astype(BF16)

    igr[c] = igs[c]
    for q in peers:
        copy(igs.at[q], igr.at[q], ig_send.at[q], ig_recv.at[q], to_chan(q)).wait_recv()
    for h in range(rows):
        at = slice(h * cols, (h + 1) * cols)
        total = igr[0, :, at]
        for q in range(1, chans):
            total = total + igr[q, :, at]
        tmp[:c_loc, h, :] = total
    ig[:, 0] = tmp[:c_loc].astype(BF16)

    def spread(buf, count, taps):
        per = buf.shape[1]
        for k in range(count):
            a, j, o = taps[k * 8 // (3 * o_loc)], (k * 8 // o_loc) % 3, k * 8 % o_loc
            m = count + k // 2
            low = buf[k // per, k % per]
            kg[a, 2 - j, 0, o:o + 8, :] = low[:, 0:c_in]
            kg[a, 2 - j, 1, o:o + 8, :] = low[:, c_in:2 * c_in]
            at = (k % 2) * c_in
            kg[a, 2 - j, 2, o:o + 8, :] = buf[m // per, m % per, :, at:at + c_in]

    if packed:
        for t in others:
            ag_from(a1, a1_send, a1_recv, t).wait_recv()
        spread(a1, 3 * o_loc // 8, (1,))
        k = (3 * o_loc // 8) * 3 // 2
        bg[...] = a1[k // a1.shape[1], k % a1.shape[1], 0:1, 0:o_loc]
        for t in others:
            ag_from(a2, a2_send, a2_recv, t).wait_recv()
        spread(a2, half // 8, (0, 2))

    for d in v_first(1) + v_relay(1):
        d.wait_send()

    @pl.when(has_next)
    def _():
        g_up.wait_send()
        v_up.wait_send()
        for d in v_first(2) + v_relay(2):
            d.wait_send()

    @pl.when(has_prev)
    def _():
        g_down.wait_send()
        v_down.wait_send()
        for d in v_first(0) + v_relay(0):
            d.wait_send()

    for d in ig_out:
        d.wait_send()
    for t in others:
        rs_copy(s1, r1, s1_send, s1_recv, t).wait_send()
        ag_copy(a1, a1_send, a1_recv, t).wait_send()
        rs_copy(s2, r2, s2_send, s2_recv, t).wait_send()
        ag_copy(a2, a2_send, a2_recv, t).wait_send()


def hand_out(feat, ig, kg, bg, feat_o, ig_o, kg_o, bg_o, sems):
    moves = [pltpu.make_async_copy(src, dst, sems.at[k]) for k, (src, dst) in enumerate(
        ((kg, kg_o), (feat, feat_o), (ig, ig_o), (bg, bg_o)))]
    for move in moves:
        move.start()
    for move in moves:
        move.wait()


def on_device(slabs, chans, volume, kernel, bias, out_grad):
    c_loc, _, rows, cols = volume.shape
    c_in, o_loc = kernel.shape[3], kernel.shape[4]
    cells = rows * cols
    packed = o_loc == 32 and c_in == 64 and slabs == 8
    scale = 1.0 / math.sqrt(slabs * cells)
    vmem = pl.BlockSpec(memory_space=pltpu.VMEM)
    parts = slabs if packed else 1
    dma = pltpu.SemaphoreType.DMA
    shapes = (
        jax.ShapeDtypeStruct((o_loc, 1, rows, cols), BF16),
        jax.ShapeDtypeStruct((c_loc, 1, rows, cols), BF16),
        jax.ShapeDtypeStruct((3, 3, 3, o_loc, c_in), F32),
        jax.ShapeDtypeStruct((1, o_loc), F32),
    )
    results = pl.pallas_call(
        functools.partial(body, slabs, chans, packed, scale),
        out_shape=shapes,
        in_specs=[vmem] * 4,
        out_specs=(vmem,) * 4,
        scratch_shapes=[
            pltpu.VMEM((max(o_loc, c_loc), rows, cols), F32),
            pltpu.VMEM((3, chans, c_loc, cells), BF16),
            pltpu.VMEM((3, o_loc, cells), BF16),
            pltpu.VMEM((9 * c_in, cells), BF16),
            pltpu.VMEM((9 * o_loc, cells), BF16),
            pltpu.VMEM((3 * c_in, cells), BF16),
            pltpu.VMEM((3 * o_loc, 9 * c_in), BF16),
            pltpu.VMEM((3 * c_in, 9 * o_loc), BF16),
            pltpu.VMEM((chans, c_loc, cells), F32),
            pltpu.VMEM((chans, c_loc, cells), F32),
            pltpu.VMEM((9 * o_loc, 256), F32),
        ] + [pltpu.VMEM((parts, 3, 8, 128), F32)] * 3 + [pltpu.VMEM((parts, 5, 8, 128), F32)] * 3
        + [dma((3, chans)), dma((3, chans)), dma((2,)), dma((2,)), dma((3,)),
           dma((chans,)), dma((chans,))] + [dma((parts,))] * 8,
        compiler_params=pltpu.CompilerParams(
            collective_id=0, has_side_effects=True, vmem_limit_bytes=40 * 1024 * 1024),
        cost_estimate=pl.CostEstimate(
            flops=3 * 2 * cells * 27 * c_in * o_loc, bytes_accessed=2 * 1024 * 1024,
            transcendentals=0),
    )(volume, jnp.swapaxes(kernel, 3, 4), bias.reshape(1, o_loc), out_grad)
    feature, input_grad, kernel_grad, bias_grad = pl.pallas_call(
        hand_out,
        out_shape=shapes,
        in_specs=[vmem] * 4,
        out_specs=(pl.BlockSpec(memory_space=pl.ANY),) * 4,
        scratch_shapes=[dma((4,))],
        compiler_params=pltpu.CompilerParams(vmem_limit_bytes=8 * 1024 * 1024),
        cost_estimate=pl.CostEstimate(flops=0, bytes_accessed=1024 * 1024, transcendentals=0),
    )(*results)
    bias_grad = bias_grad.reshape(o_loc)
    kernel_grad = jnp.swapaxes(kernel_grad, 3, 4)
    if not packed:
        kernel_grad, bias_grad = lax.psum((kernel_grad, bias_grad), "slab")
        kernel_grad, bias_grad = kernel_grad * scale, bias_grad * scale
    return feature, input_grad, kernel_grad, bias_grad


def solution(mesh):
    specs = (
        P("chan", "slab", None, None),
        P(None, None, None, None, "chan"),
        P("chan"),
        P("chan", "slab", None, None),
    )
    out_specs = (specs[0], specs[0], specs[1], specs[2])
    run = functools.partial(on_device, mesh.shape["slab"], mesh.shape["chan"])
    return jax.shard_map(run, mesh=mesh, in_specs=specs, out_specs=out_specs, check_vma=False)
```

```python
import functools
import math

import jax
import jax.numpy as jnp
from jax import lax
from jax.experimental import pallas as pl
from jax.experimental.pallas import tpu as pltpu
from jax.sharding import PartitionSpec as P

F32 = jnp.float32
BF16 = jnp.bfloat16
MESH = pl.DeviceIdType.MESH


def roll_cols(value, step):
    width = value.shape[-1]
    lane = lax.broadcasted_iota(jnp.int32, value.shape, value.ndim - 1)
    edge = 0 if step > 0 else width - 1
    return jnp.where(lane == edge, 0.0, pltpu.roll(value, step % width, value.ndim - 1))


def body(slabs, chans, packed, scale, vol_in, ker_in, bias_in, og_in, feat, ig, kg, bg,
         vol, ker, bias, og, in_sem, tmp, rv, rg, xv3, xg3, vc, w1, w2, igs, igr, part,
         s1, r1, a1, s2, r2, a2,
         v_send, v_recv, vh_send, g_send, g_recv, ig_send, ig_recv,
         s1_send, s1_recv, a1_send, a1_recv, s2_send, s2_recv, a2_send, a2_recv):
    o_loc, c_in = ker.shape[3], ker.shape[4]
    c_loc, rows, cols = vol.shape[0], vol.shape[2], vol.shape[3]
    cells = rows * cols
    s = lax.axis_index("slab")
    c = lax.axis_index("chan")
    has_prev, has_next = s > 0, s < slabs - 1

    def to_slab(t):
        return {"slab": t}

    def to_chan(t):
        return {"chan": t}

    def other_core(q):
        return q + 1 - 2 * lax.rem(q, 2)

    peers = [lax.rem(c + k, chans) for k in range(1, chans)]
    sib = other_core(c)
    same = [lax.rem(c + 2 * k, chans) for k in range(1, chans // 2)]
    others = [lax.rem(s + k, slabs) for k in range(1, slabs)] if packed else []

    loads = [pltpu.make_async_copy(src, dst, in_sem.at[k]) for k, (src, dst) in enumerate(
        ((og_in, og), (vol_in, vol), (ker_in, ker), (bias_in, bias)))]
    for load in loads:
        load.start()

    barrier = pltpu.get_barrier_semaphore()
    for p in peers:
        pl.semaphore_signal(barrier, inc=1, device_id=to_chan(p), device_id_type=MESH)
    if packed:
        for t in others:
            pl.semaphore_signal(barrier, inc=1, device_id=to_slab(t), device_id_type=MESH)
    else:
        @pl.when(has_prev)
        def _():
            pl.semaphore_signal(barrier, inc=1, device_id=to_slab(s - 1), device_id_type=MESH)

        @pl.when(has_next)
        def _():
            pl.semaphore_signal(barrier, inc=1, device_id=to_slab(s + 1), device_id_type=MESH)

    loads[0].wait()
    tmp[...] = og[:, 0].astype(F32)
    for h in range(rows):
        rg[1, :, h * cols:(h + 1) * cols] = tmp[:, h, :].astype(BF16)
    loads[1].wait()
    tmp[:c_loc] = vol[:, 0].astype(F32)
    for h in range(rows):
        rv[1, c, :, h * cols:(h + 1) * cols] = tmp[:c_loc, h, :].astype(BF16)

    if packed:
        pl.semaphore_wait(barrier, chans - 1 + slabs - 1)
    else:
        pl.semaphore_wait(barrier, chans - 1)

        @pl.when(has_prev)
        def _():
            pl.semaphore_wait(barrier, 1)

        @pl.when(has_next)
        def _():
            pl.semaphore_wait(barrier, 1)

    def copy(src, dst, ssem, rsem, dev):
        return pltpu.make_async_remote_copy(
            src_ref=src, dst_ref=dst, send_sem=ssem, recv_sem=rsem,
            device_id=dev, device_id_type=MESH)

    if packed:
        x = lax.rem(s, 2)
        near, far = 2 * x, 2 - 2 * x
        has_near, pair = s >= 0, other_core(s)
        has_far = jnp.logical_and(s + 2 * x >= 2, s + 2 * x < slabs)
        relays = jnp.logical_and(s - 2 * x >= 0, s - 2 * x < slabs - 2)
        g_near = [copy(rg.at[1, pl.ds(k, o_loc // 2)], rg.at[far, pl.ds(k, o_loc // 2)],
                       g_send.at[0, i], g_recv.at[far, i], to_slab(pair))
                  for i, k in enumerate((0, o_loc // 2))]
        g_got = [copy(rg.at[1, pl.ds(k, o_loc // 2)], rg.at[near, pl.ds(k, o_loc // 2)],
                      g_send.at[0, i], g_recv.at[near, i], to_slab(pair))
                 for i, k in enumerate((0, o_loc // 2))]
        g_far = [copy(rg.at[near, pl.ds(k, o_loc // 2)], rg.at[far, pl.ds(k, o_loc // 2)],
                      g_send.at[1, i], g_recv.at[far, i], to_slab(s + 2 - 4 * x))
                 for i, k in enumerate((0, o_loc // 2))]
        vn, vf = far, near
        v_near = copy(rv.at[1, c], rv.at[vf, c], vh_send.at[0], v_recv.at[vf, c], to_slab(pair))
        v_got = copy(rv.at[1, c], rv.at[vn, c], vh_send.at[0], v_recv.at[vn, c], to_slab(pair))
        v_far = copy(rv.at[vn, c], rv.at[vf, c], vh_send.at[1], v_recv.at[vf, c],
                     to_slab(s + 2 - 4 * x))
    else:
        g_up = copy(rg.at[1], rg.at[2], g_send.at[0, 0], g_recv.at[2, 0], to_slab(s + 1))
        g_down = copy(rg.at[1], rg.at[0], g_send.at[1, 0], g_recv.at[0, 0], to_slab(s - 1))
        v_up = copy(rv.at[1, c], rv.at[0, c], vh_send.at[0], v_recv.at[0, c], to_slab(s + 1))
        v_down = copy(rv.at[1, c], rv.at[2, c], vh_send.at[1], v_recv.at[2, c], to_slab(s - 1))

    def relay_g(i):
        if packed:
            g_got[i].wait_recv()

            @pl.when(relays)
            def _():
                g_far[i].start()

    def v_block(a, q, p, slot):
        return copy(rv.at[a, q], rv.at[a, q], v_send.at[a, slot], v_recv.at[a, q], to_chan(p))

    def v_first(a):
        return [v_block(a, c, p, p) for p in same] + [v_block(a, c, sib, sib)]

    def v_relay(a):
        return [v_block(a, q, sib, other_core(q)) for q in same]

    def v_relay_wait(a):
        for q, d in zip(same, v_relay(a)):
            v_block(a, q, sib, other_core(q)).wait_recv()
            d.start()

    def v_rest_wait(a):
        for q in [sib] + [other_core(q) for q in same]:
            v_block(a, q, sib, q).wait_recv()

    for d in v_first(1):
        d.start()

    if packed:
        for d in g_near:
            d.start()
    else:
        @pl.when(has_next)
        def _():
            g_up.start()

        @pl.when(has_prev)
        def _():
            g_down.start()

    loads[2].wait()
    loads[3].wait()
    order = (0, 2, 1)
    w2t = jnp.concatenate(
        [jnp.concatenate([ker[a, 2 - j, cc].astype(F32) for cc in range(3)], axis=1)
         for a in order for j in range(3)], axis=0)
    w2[...] = jnp.transpose(w2t).astype(BF16)
    for cc in range(3):
        w1[cc * o_loc:(cc + 1) * o_loc, :] = jnp.concatenate(
            [ker[a, b, cc].astype(F32) for a in range(3) for b in range(3)], axis=1
        ).astype(BF16)

    def windows(dst, base, block):
        n = block.shape[0]
        zero = jnp.zeros((n, cols), BF16)
        at = base * 3 * n
        dst[at:at + n, 0:cols] = zero
        dst[at:at + n, cols:cells] = block[:, 0:cells - cols]
        dst[at + n:at + 2 * n, :] = block
        dst[at + 2 * n:at + 3 * n, 0:cells - cols] = block[:, cols:cells]
        dst[at + 2 * n:at + 3 * n, cells - cols:cells] = zero

    windows(xg3, 2, rg[1])
    nt = (((1,), (1,)), ((), ()))
    bias_part = lax.dot_general(
        jnp.ones((8, cells), BF16), rg[1], nt, preferred_element_type=F32)

    v_relay_wait(1)
    relay_g(0)
    v_rest_wait(1)
    v_own = jnp.concatenate([rv[1, q] for q in range(chans)], axis=0)
    for h in range(rows):
        at = slice(h * cols, (h + 1) * cols)
        block = v_own[:, at]
        wide = block.astype(F32)
        vc[0:c_in, at] = roll_cols(wide, 1).astype(BF16)
        vc[c_in:2 * c_in, at] = block
        vc[2 * c_in:3 * c_in, at] = roll_cols(wide, -1).astype(BF16)

    relay_g(1)
    if packed:
        v_near.start()
    else:
        @pl.when(has_next)
        def _():
            v_up.start()

        @pl.when(has_prev)
        def _():
            v_down.start()

    half = 6 * o_loc
    wide_to = 3 * c_in
    part[half:, 0:wide_to] = lax.dot_general(
        xg3[half:, :], vc[...], nt, preferred_element_type=F32)

    def tiles(start, count):
        found = [part[start + 8 * k:start + 8 * k + 8, 0:128] for k in range(count)]
        for k in range(0, count, 2):
            found.append(jnp.concatenate(
                [part[start + 8 * k:start + 8 * k + 8, 128:192],
                 part[start + 8 * k + 8:start + 8 * k + 16, 128:192]], axis=1))
        return found

    def fill(dst, found):
        per = dst.shape[1]
        found = found + [jnp.zeros((8, 128), F32)] * (per * slabs - len(found))
        for k, tile in enumerate(found):
            dst[k // per, k % per] = tile

    def rs_copy(src, dst, ssem, rsem, t):
        return copy(src.at[t], dst.at[s], ssem.at[t], rsem.at[s], to_slab(t))

    def rs_from(src, dst, ssem, rsem, t):
        return copy(src.at[t], dst.at[t], ssem.at[t], rsem.at[t], to_slab(t))

    def ag_copy(buf, ssem, rsem, t):
        return copy(buf.at[s], buf.at[s], ssem.at[t], rsem.at[s], to_slab(t))

    def ag_from(buf, ssem, rsem, t):
        return copy(buf.at[t], buf.at[t], ssem.at[t], rsem.at[t], to_slab(t))

    def reduce_rows(src, dst, buf, ssem, rsem):
        dst[s] = src[s]
        for t in others:
            rs_from(src, dst, ssem, rsem, t).wait_recv()
        done = dst[0]
        for t in range(1, slabs):
            done = done + dst[t]
        buf[s] = done * scale

    if packed:
        fill(s1, tiles(half, 3 * o_loc // 8)
             + [jnp.concatenate([bias_part, jnp.zeros((8, 128 - o_loc), F32)], axis=1)])
        for t in others:
            rs_copy(s1, r1, s1_send, s1_recv, t).start()

    if packed:
        @pl.when(has_far)
        def _():
            for d in g_far:
                d.wait_recv()
    else:
        @pl.when(has_next)
        def _():
            g_down.wait_recv()

        @pl.when(has_prev)
        def _():
            g_up.wait_recv()

    @pl.when(jnp.logical_not(has_next))
    def _():
        rg[0] = jnp.zeros((o_loc, cells), BF16)

    windows(xg3, 0, rg[0])

    @pl.when(jnp.logical_not(has_prev))
    def _():
        rg[2] = jnp.zeros((o_loc, cells), BF16)

    windows(xg3, 1, rg[2])
    part[0:half, 0:wide_to] = lax.dot_general(
        xg3[0:half, :], vc[...], nt, preferred_element_type=F32)
    if packed:
        fill(s2, tiles(0, half // 8))
        for t in others:
            rs_copy(s2, r2, s2_send, s2_recv, t).start()

    if packed:
        v_got.wait_recv()

        @pl.when(relays)
        def _():
            v_far.start()

        for d in v_first(vn):
            d.start()
        reduce_rows(s1, r1, a1, s1_send, s1_recv)
        for t in others:
            ag_copy(a1, a1_send, a1_recv, t).start()
    else:
        @pl.when(has_prev)
        def _():
            v_up.wait_recv()
            for d in v_first(0):
                d.start()

        @pl.when(has_next)
        def _():
            v_down.wait_recv()
            for d in v_first(2):
                d.start()

    share = jnp.dot(w2[...], xg3[...], preferred_element_type=F32)
    for h in range(rows):
        at = slice(h * cols, (h + 1) * cols)
        total = (share[c_in:2 * c_in, at] + roll_cols(share[0:c_in, at], -1)
                 + roll_cols(share[2 * c_in:3 * c_in, at], 1))
        for p in range(chans):
            igs[p, :, at] = total[p * c_loc:(p + 1) * c_loc]
    ig_out = [copy(igs.at[p], igr.at[c], ig_send.at[p], ig_recv.at[c], to_chan(p)) for p in peers]
    for d in ig_out:
        d.start()

    if packed:
        @pl.when(has_far)
        def _():
            v_far.wait_recv()
            for d in v_first(vf):
                d.start()

        v_relay_wait(vn)
    else:
        @pl.when(has_prev)
        def _():
            v_relay_wait(0)

        @pl.when(has_next)
        def _():
            v_relay_wait(2)

    if packed:
        reduce_rows(s2, r2, a2, s2_send, s2_recv)
        for t in others:
            ag_copy(a2, a2_send, a2_recv, t).start()

        @pl.when(has_far)
        def _():
            v_relay_wait(vf)
    else:
        bg[...] = bias_part[0:1, :]
        for k, a in enumerate(order):
            for j in range(3):
                for cc in range(3):
                    at = (k * 3 + j) * o_loc
                    kg[a, 2 - j, cc] = part[at:at + o_loc, cc * c_in:(cc + 1) * c_in]

    windows(xv3, 1, v_own)
    for a, here in ((0, has_prev), (2, has_next)):
        @pl.when(here)
        def _():
            v_rest_wait(a)

        @pl.when(jnp.logical_not(here))
        def _():
            rv[a] = jnp.zeros((chans, c_loc, cells), BF16)

        windows(xv3, a, jnp.concatenate([rv[a, q] for q in range(chans)], axis=0))
    pre = jnp.dot(w1[...], xv3[...], preferred_element_type=F32)
    bias_col = jnp.transpose(jnp.broadcast_to(bias[...], (cols, o_loc)))
    for h in range(rows):
        at = slice(h * cols, (h + 1) * cols)
        tmp[:, h, :] = (pre[o_loc:2 * o_loc, at] + roll_cols(pre[0:o_loc, at], 1)
                        + roll_cols(pre[2 * o_loc:3 * o_loc, at], -1) + bias_col)
    feat[:, 0] = tmp[...].astype(BF16)

    igr[c] = igs[c]
    for q in peers:
        copy(igs.at[q], igr.at[q], ig_send.at[q], ig_recv.at[q], to_chan(q)).wait_recv()
    for h in range(rows):
        at = slice(h * cols, (h + 1) * cols)
        total = igr[0, :, at]
        for q in range(1, chans):
            total = total + igr[q, :, at]
        tmp[:c_loc, h, :] = total
    ig[:, 0] = tmp[:c_loc].astype(BF16)

    def spread(buf, count, taps):
        per = buf.shape[1]
        for k in range(count):
            a, j, o = taps[k * 8 // (3 * o_loc)], (k * 8 // o_loc) % 3, k * 8 % o_loc
            m = count + k // 2
            low = buf[k // per, k % per]
            kg[a, 2 - j, 0, o:o + 8, :] = low[:, 0:c_in]
            kg[a, 2 - j, 1, o:o + 8, :] = low[:, c_in:2 * c_in]
            at = (k % 2) * c_in
            kg[a, 2 - j, 2, o:o + 8, :] = buf[m // per, m % per, :, at:at + c_in]

    if packed:
        for t in others:
            ag_from(a1, a1_send, a1_recv, t).wait_recv()
        spread(a1, 3 * o_loc // 8, (1,))
        k = (3 * o_loc // 8) * 3 // 2
        bg[...] = a1[k // a1.shape[1], k % a1.shape[1], 0:1, 0:o_loc]
        for t in others:
            ag_from(a2, a2_send, a2_recv, t).wait_recv()
        spread(a2, half // 8, (0, 2))

    for d in v_first(1) + v_relay(1):
        d.wait_send()

    if packed:
        for d in g_near + [v_near]:
            d.wait_send()

        @pl.when(relays)
        def _():
            for d in g_far + [v_far]:
                d.wait_send()
    else:
        @pl.when(has_next)
        def _():
            g_up.wait_send()
            v_up.wait_send()

        @pl.when(has_prev)
        def _():
            g_down.wait_send()
            v_down.wait_send()

    @pl.when(has_next)
    def _():
        for d in v_first(2) + v_relay(2):
            d.wait_send()

    @pl.when(has_prev)
    def _():
        for d in v_first(0) + v_relay(0):
            d.wait_send()

    for d in ig_out:
        d.wait_send()
    for t in others:
        rs_copy(s1, r1, s1_send, s1_recv, t).wait_send()
        ag_copy(a1, a1_send, a1_recv, t).wait_send()
        rs_copy(s2, r2, s2_send, s2_recv, t).wait_send()
        ag_copy(a2, a2_send, a2_recv, t).wait_send()


def hand_out(feat, ig, kg, bg, feat_o, ig_o, kg_o, bg_o, sems):
    moves = [pltpu.make_async_copy(src, dst, sems.at[k]) for k, (src, dst) in enumerate(
        ((kg, kg_o), (feat, feat_o), (ig, ig_o), (bg, bg_o)))]
    for move in moves:
        move.start()
    for move in moves:
        move.wait()


def on_device(slabs, chans, volume, kernel, bias, out_grad):
    c_loc, _, rows, cols = volume.shape
    c_in, o_loc = kernel.shape[3], kernel.shape[4]
    cells = rows * cols
    packed = o_loc == 32 and c_in == 64 and slabs == 8
    scale = 1.0 / math.sqrt(slabs * cells)
    vmem = pl.BlockSpec(memory_space=pltpu.VMEM)
    parts = slabs if packed else 1
    dma = pltpu.SemaphoreType.DMA
    shapes = (
        jax.ShapeDtypeStruct((o_loc, 1, rows, cols), BF16),
        jax.ShapeDtypeStruct((c_loc, 1, rows, cols), BF16),
        jax.ShapeDtypeStruct((3, 3, 3, o_loc, c_in), F32),
        jax.ShapeDtypeStruct((1, o_loc), F32),
    )
    results = pl.pallas_call(
        functools.partial(body, slabs, chans, packed, scale),
        out_shape=shapes,
        in_specs=[pl.BlockSpec(memory_space=pltpu.HBM)] * 4,
        out_specs=(vmem,) * 4,
        scratch_shapes=[
            pltpu.VMEM(volume.shape, BF16),
            pltpu.VMEM((3, 3, 3, o_loc, c_in), BF16),
            pltpu.VMEM((1, o_loc), F32),
            pltpu.VMEM(out_grad.shape, BF16),
            dma((4,)),
            pltpu.VMEM((max(o_loc, c_loc), rows, cols), F32),
            pltpu.VMEM((3, chans, c_loc, cells), BF16),
            pltpu.VMEM((3, o_loc, cells), BF16),
            pltpu.VMEM((9 * c_in, cells), BF16),
            pltpu.VMEM((9 * o_loc, cells), BF16),
            pltpu.VMEM((3 * c_in, cells), BF16),
            pltpu.VMEM((3 * o_loc, 9 * c_in), BF16),
            pltpu.VMEM((3 * c_in, 9 * o_loc), BF16),
            pltpu.VMEM((chans, c_loc, cells), F32),
            pltpu.VMEM((chans, c_loc, cells), F32),
            pltpu.VMEM((9 * o_loc, 256), F32),
        ] + [pltpu.VMEM((parts, 3, 8, 128), F32)] * 3 + [pltpu.VMEM((parts, 5, 8, 128), F32)] * 3
        + [dma((3, chans)), dma((3, chans)), dma((2,)), dma((2, 2)), dma((3, 2)),
           dma((chans,)), dma((chans,))] + [dma((parts,))] * 8,
        compiler_params=pltpu.CompilerParams(
            collective_id=0, has_side_effects=True, vmem_limit_bytes=64 * 1024 * 1024),
        cost_estimate=pl.CostEstimate(
            flops=3 * 2 * cells * 27 * c_in * o_loc, bytes_accessed=2 * 1024 * 1024,
            transcendentals=0),
    )(volume, jnp.swapaxes(kernel, 3, 4), bias.reshape(1, o_loc), out_grad)
    feature, input_grad, kernel_grad, bias_grad = pl.pallas_call(
        hand_out,
        out_shape=shapes,
        in_specs=[pl.BlockSpec(memory_space=pl.ANY)] * 4,
        out_specs=(pl.BlockSpec(memory_space=pl.ANY),) * 4,
        scratch_shapes=[dma((4,))],
        compiler_params=pltpu.CompilerParams(vmem_limit_bytes=64 * 1024 * 1024),
        cost_estimate=pl.CostEstimate(flops=0, bytes_accessed=1024 * 1024, transcendentals=0),
    )(*results)
    bias_grad = bias_grad.reshape(o_loc)
    kernel_grad = jnp.swapaxes(kernel_grad, 3, 4)
    if not packed:
        kernel_grad, bias_grad = lax.psum((kernel_grad, bias_grad), "slab")
        kernel_grad, bias_grad = kernel_grad * scale, bias_grad * scale
    return feature, input_grad, kernel_grad, bias_grad


def solution(mesh):
    specs = (
        P("chan", "slab", None, None),
        P(None, None, None, None, "chan"),
        P("chan"),
        P("chan", "slab", None, None),
    )
    out_specs = (specs[0], specs[0], specs[1], specs[2])
    run = functools.partial(on_device, mesh.shape["slab"], mesh.shape["chan"])
    return jax.shard_map(run, mesh=mesh, in_specs=specs, out_specs=out_specs, check_vma=False)
```

```python
import functools
import math

import jax
import jax.numpy as jnp
from jax import lax
from jax.experimental import pallas as pl
from jax.experimental.pallas import tpu as pltpu
from jax.sharding import PartitionSpec as P

F32 = jnp.float32
BF16 = jnp.bfloat16
MESH = pl.DeviceIdType.MESH


def roll_cols(value, step):
    width = value.shape[-1]
    lane = lax.broadcasted_iota(jnp.int32, value.shape, value.ndim - 1)
    edge = 0 if step > 0 else width - 1
    return jnp.where(lane == edge, 0.0, pltpu.roll(value, step % width, value.ndim - 1))


def body(slabs, chans, packed, scale, vol_in, ker_in, bias_in, og_in, feat, ig, kg, bg,
         vol, ker, bias, og, in_sem, tmp, rv, rg, xv3, xg3, vc, w1, w2, igs, igr, part,
         s1, r1, a1, s2, r2, a2,
         v_send, v_recv, vh_send, g_send, g_recv, ig_send, ig_recv,
         s1_send, s1_recv, a1_send, a1_recv, s2_send, s2_recv, a2_send, a2_recv):
    o_loc, c_in = ker.shape[3], ker.shape[4]
    c_loc, rows, cols = vol.shape[0], vol.shape[2], vol.shape[3]
    cells = rows * cols
    s = lax.axis_index("slab")
    c = lax.axis_index("chan")
    has_prev, has_next = s > 0, s < slabs - 1

    def to_slab(t):
        return {"slab": t}

    def to_chan(t):
        return {"chan": t}

    def other_core(q):
        return q + 1 - 2 * lax.rem(q, 2)

    peers = [lax.rem(c + k, chans) for k in range(1, chans)]
    sib = other_core(c)
    same = [lax.rem(c + 2 * k, chans) for k in range(1, chans // 2)]
    others = [lax.rem(s + k, slabs) for k in range(1, slabs)] if packed else []

    loads = [pltpu.make_async_copy(src, dst, in_sem.at[k]) for k, (src, dst) in enumerate(
        ((og_in, og), (vol_in, vol), (ker_in, ker), (bias_in, bias)))]
    for load in loads:
        load.start()

    barrier = pltpu.get_barrier_semaphore()
    for p in peers:
        pl.semaphore_signal(barrier, inc=1, device_id=to_chan(p), device_id_type=MESH)
    if packed:
        for t in others:
            pl.semaphore_signal(barrier, inc=1, device_id=to_slab(t), device_id_type=MESH)
    else:
        @pl.when(has_prev)
        def _():
            pl.semaphore_signal(barrier, inc=1, device_id=to_slab(s - 1), device_id_type=MESH)

        @pl.when(has_next)
        def _():
            pl.semaphore_signal(barrier, inc=1, device_id=to_slab(s + 1), device_id_type=MESH)

    loads[0].wait()
    tmp[...] = og[:, 0].astype(F32)
    for h in range(rows):
        rg[1, :, h * cols:(h + 1) * cols] = tmp[:, h, :].astype(BF16)
    loads[1].wait()
    tmp[:c_loc] = vol[:, 0].astype(F32)
    for h in range(rows):
        rv[1, c, :, h * cols:(h + 1) * cols] = tmp[:c_loc, h, :].astype(BF16)

    if packed:
        pl.semaphore_wait(barrier, chans - 1 + slabs - 1)
    else:
        pl.semaphore_wait(barrier, chans - 1)

        @pl.when(has_prev)
        def _():
            pl.semaphore_wait(barrier, 1)

        @pl.when(has_next)
        def _():
            pl.semaphore_wait(barrier, 1)

    def copy(src, dst, ssem, rsem, dev):
        return pltpu.make_async_remote_copy(
            src_ref=src, dst_ref=dst, send_sem=ssem, recv_sem=rsem,
            device_id=dev, device_id_type=MESH)

    if packed:
        x = lax.rem(s, 2)
        near, far = 2 * x, 2 - 2 * x
        has_near, pair = s >= 0, other_core(s)
        has_far = jnp.logical_and(s + 2 * x >= 2, s + 2 * x < slabs)
        relays = jnp.logical_and(s - 2 * x >= 0, s - 2 * x < slabs - 2)
        g_near = [copy(rg.at[1, pl.ds(k, o_loc // 2)], rg.at[far, pl.ds(k, o_loc // 2)],
                       g_send.at[0, i], g_recv.at[far, i], to_slab(pair))
                  for i, k in enumerate((0, o_loc // 2))]
        g_got = [copy(rg.at[1, pl.ds(k, o_loc // 2)], rg.at[near, pl.ds(k, o_loc // 2)],
                      g_send.at[0, i], g_recv.at[near, i], to_slab(pair))
                 for i, k in enumerate((0, o_loc // 2))]
        g_far = [copy(rg.at[near, pl.ds(k, o_loc // 2)], rg.at[far, pl.ds(k, o_loc // 2)],
                      g_send.at[1, i], g_recv.at[far, i], to_slab(s + 2 - 4 * x))
                 for i, k in enumerate((0, o_loc // 2))]
        vn, vf = far, near
        v_near = copy(rv.at[1, c], rv.at[vf, c], vh_send.at[0], v_recv.at[vf, c], to_slab(pair))
        v_got = copy(rv.at[1, c], rv.at[vn, c], vh_send.at[0], v_recv.at[vn, c], to_slab(pair))
        v_far = copy(rv.at[vn, c], rv.at[vf, c], vh_send.at[1], v_recv.at[vf, c],
                     to_slab(s + 2 - 4 * x))
    else:
        g_up = copy(rg.at[1], rg.at[2], g_send.at[0, 0], g_recv.at[2, 0], to_slab(s + 1))
        g_down = copy(rg.at[1], rg.at[0], g_send.at[1, 0], g_recv.at[0, 0], to_slab(s - 1))
        v_up = copy(rv.at[1, c], rv.at[0, c], vh_send.at[0], v_recv.at[0, c], to_slab(s + 1))
        v_down = copy(rv.at[1, c], rv.at[2, c], vh_send.at[1], v_recv.at[2, c], to_slab(s - 1))

    def relay_g(i):
        if packed:
            g_got[i].wait_recv()

            @pl.when(relays)
            def _():
                g_far[i].start()

    def v_block(a, q, p, slot):
        return copy(rv.at[a, q], rv.at[a, q], v_send.at[a, slot], v_recv.at[a, q], to_chan(p))

    def v_first(a):
        return [v_block(a, c, p, p) for p in same] + [v_block(a, c, sib, sib)]

    def v_relay(a):
        return [v_block(a, q, sib, other_core(q)) for q in same]

    def v_relay_wait(a):
        for q, d in zip(same, v_relay(a)):
            v_block(a, q, sib, other_core(q)).wait_recv()
            d.start()

    def v_rest_wait(a):
        for q in [sib] + [other_core(q) for q in same]:
            v_block(a, q, sib, q).wait_recv()

    for d in v_first(1):
        d.start()

    if packed:
        for d in g_near:
            d.start()
    else:
        @pl.when(has_next)
        def _():
            g_up.start()

        @pl.when(has_prev)
        def _():
            g_down.start()

    loads[2].wait()
    loads[3].wait()
    order = (0, 2, 1)
    w2t = jnp.concatenate(
        [jnp.concatenate([ker[a, 2 - j, cc].astype(F32) for cc in range(3)], axis=1)
         for a in order for j in range(3)], axis=0)
    w2[...] = jnp.transpose(w2t).astype(BF16)
    for cc in range(3):
        w1[cc * o_loc:(cc + 1) * o_loc, :] = jnp.concatenate(
            [ker[a, b, cc].astype(F32) for a in range(3) for b in range(3)], axis=1
        ).astype(BF16)

    def windows(dst, base, block):
        n = block.shape[0]
        zero = jnp.zeros((n, cols), BF16)
        at = base * 3 * n
        dst[at:at + n, 0:cols] = zero
        dst[at:at + n, cols:cells] = block[:, 0:cells - cols]
        dst[at + n:at + 2 * n, :] = block
        dst[at + 2 * n:at + 3 * n, 0:cells - cols] = block[:, cols:cells]
        dst[at + 2 * n:at + 3 * n, cells - cols:cells] = zero

    windows(xg3, 2, rg[1])
    nt = (((1,), (1,)), ((), ()))
    bias_part = lax.dot_general(
        jnp.ones((8, cells), BF16), rg[1], nt, preferred_element_type=F32)

    v_relay_wait(1)
    relay_g(0)
    v_rest_wait(1)
    v_own = jnp.concatenate([rv[1, q] for q in range(chans)], axis=0)
    for h in range(rows):
        at = slice(h * cols, (h + 1) * cols)
        block = v_own[:, at]
        wide = block.astype(F32)
        vc[0:c_in, at] = roll_cols(wide, 1).astype(BF16)
        vc[c_in:2 * c_in, at] = block
        vc[2 * c_in:3 * c_in, at] = roll_cols(wide, -1).astype(BF16)

    relay_g(1)
    if packed:
        v_near.start()
    else:
        @pl.when(has_next)
        def _():
            v_up.start()

        @pl.when(has_prev)
        def _():
            v_down.start()

    half = 6 * o_loc
    wide_to = 3 * c_in
    part[half:, 0:wide_to] = lax.dot_general(
        xg3[half:, :], vc[...], nt, preferred_element_type=F32)

    def tiles(start, count):
        found = [part[start + 8 * k:start + 8 * k + 8, 0:128] for k in range(count)]
        for k in range(0, count, 2):
            found.append(jnp.concatenate(
                [part[start + 8 * k:start + 8 * k + 8, 128:192],
                 part[start + 8 * k + 8:start + 8 * k + 16, 128:192]], axis=1))
        return found

    def fill(dst, found):
        per = dst.shape[1]
        found = found + [jnp.zeros((8, 128), F32)] * (per * slabs - len(found))
        for k, tile in enumerate(found):
            dst[k // per, k % per] = tile

    def rs_copy(src, dst, ssem, rsem, t):
        return copy(src.at[t], dst.at[s], ssem.at[t], rsem.at[s], to_slab(t))

    def rs_from(src, dst, ssem, rsem, t):
        return copy(src.at[t], dst.at[t], ssem.at[t], rsem.at[t], to_slab(t))

    def ag_copy(buf, ssem, rsem, t):
        return copy(buf.at[s], buf.at[s], ssem.at[t], rsem.at[s], to_slab(t))

    def ag_from(buf, ssem, rsem, t):
        return copy(buf.at[t], buf.at[t], ssem.at[t], rsem.at[t], to_slab(t))

    def reduce_rows(src, dst, buf, ssem, rsem):
        dst[s] = src[s]
        for t in others:
            rs_from(src, dst, ssem, rsem, t).wait_recv()
        done = dst[0]
        for t in range(1, slabs):
            done = done + dst[t]
        buf[s] = done * scale

    if packed:
        fill(s1, tiles(half, 3 * o_loc // 8)
             + [jnp.concatenate([bias_part, jnp.zeros((8, 128 - o_loc), F32)], axis=1)])
        for t in others:
            rs_copy(s1, r1, s1_send, s1_recv, t).start()

    if packed:
        @pl.when(has_far)
        def _():
            for d in g_far:
                d.wait_recv()
    else:
        @pl.when(has_next)
        def _():
            g_down.wait_recv()

        @pl.when(has_prev)
        def _():
            g_up.wait_recv()

    @pl.when(jnp.logical_not(has_next))
    def _():
        rg[0] = jnp.zeros((o_loc, cells), BF16)

    windows(xg3, 0, rg[0])

    @pl.when(jnp.logical_not(has_prev))
    def _():
        rg[2] = jnp.zeros((o_loc, cells), BF16)

    windows(xg3, 1, rg[2])
    part[0:half, 0:wide_to] = lax.dot_general(
        xg3[0:half, :], vc[...], nt, preferred_element_type=F32)
    if packed:
        fill(s2, tiles(0, half // 8))
        for t in others:
            rs_copy(s2, r2, s2_send, s2_recv, t).start()

    if packed:
        v_got.wait_recv()

        @pl.when(relays)
        def _():
            v_far.start()

        for d in v_first(vn):
            d.start()
        reduce_rows(s1, r1, a1, s1_send, s1_recv)
        for t in others:
            ag_copy(a1, a1_send, a1_recv, t).start()
    else:
        @pl.when(has_prev)
        def _():
            v_up.wait_recv()
            for d in v_first(0):
                d.start()

        @pl.when(has_next)
        def _():
            v_down.wait_recv()
            for d in v_first(2):
                d.start()

    share = jnp.dot(w2[...], xg3[...], preferred_element_type=F32)
    for h in range(rows):
        at = slice(h * cols, (h + 1) * cols)
        total = (share[c_in:2 * c_in, at] + roll_cols(share[0:c_in, at], -1)
                 + roll_cols(share[2 * c_in:3 * c_in, at], 1))
        for p in range(chans):
            igs[p, :, at] = total[p * c_loc:(p + 1) * c_loc]
    ig_out = [copy(igs.at[p], igr.at[c], ig_send.at[p], ig_recv.at[c], to_chan(p)) for p in peers]
    for d in ig_out:
        d.start()

    if packed:
        @pl.when(has_far)
        def _():
            v_far.wait_recv()
            for d in v_first(vf):
                d.start()

        v_relay_wait(vn)
    else:
        @pl.when(has_prev)
        def _():
            v_relay_wait(0)

        @pl.when(has_next)
        def _():
            v_relay_wait(2)

    if packed:
        reduce_rows(s2, r2, a2, s2_send, s2_recv)
        for t in others:
            ag_copy(a2, a2_send, a2_recv, t).start()

        @pl.when(has_far)
        def _():
            v_relay_wait(vf)
    else:
        bg[...] = bias_part[0:1, :]
        for k, a in enumerate(order):
            for j in range(3):
                for cc in range(3):
                    at = (k * 3 + j) * o_loc
                    kg[a, 2 - j, cc] = part[at:at + o_loc, cc * c_in:(cc + 1) * c_in]

    windows(xv3, 1, v_own)
    for a, here in ((0, has_prev), (2, has_next)):
        @pl.when(here)
        def _():
            v_rest_wait(a)

        @pl.when(jnp.logical_not(here))
        def _():
            rv[a] = jnp.zeros((chans, c_loc, cells), BF16)

        windows(xv3, a, jnp.concatenate([rv[a, q] for q in range(chans)], axis=0))
    pre = jnp.dot(w1[...], xv3[...], preferred_element_type=F32)
    bias_col = jnp.transpose(jnp.broadcast_to(bias[...], (cols, o_loc)))
    for h in range(rows):
        at = slice(h * cols, (h + 1) * cols)
        tmp[:, h, :] = (pre[o_loc:2 * o_loc, at] + roll_cols(pre[0:o_loc, at], 1)
                        + roll_cols(pre[2 * o_loc:3 * o_loc, at], -1) + bias_col)
    feat[:, 0] = tmp[...].astype(BF16)

    igr[c] = igs[c]
    for q in peers:
        copy(igs.at[q], igr.at[q], ig_send.at[q], ig_recv.at[q], to_chan(q)).wait_recv()
    for h in range(rows):
        at = slice(h * cols, (h + 1) * cols)
        total = igr[0, :, at]
        for q in range(1, chans):
            total = total + igr[q, :, at]
        tmp[:c_loc, h, :] = total
    ig[:, 0] = tmp[:c_loc].astype(BF16)

    def spread(buf, count, taps):
        per = buf.shape[1]
        for k in range(count):
            a, j, o = taps[k * 8 // (3 * o_loc)], (k * 8 // o_loc) % 3, k * 8 % o_loc
            m = count + k // 2
            low = buf[k // per, k % per]
            kg[a, 2 - j, 0, o:o + 8, :] = low[:, 0:c_in]
            kg[a, 2 - j, 1, o:o + 8, :] = low[:, c_in:2 * c_in]
            at = (k % 2) * c_in
            kg[a, 2 - j, 2, o:o + 8, :] = buf[m // per, m % per, :, at:at + c_in]

    if packed:
        for t in others:
            ag_from(a1, a1_send, a1_recv, t).wait_recv()
        spread(a1, 3 * o_loc // 8, (1,))
        k = (3 * o_loc // 8) * 3 // 2
        bg[...] = a1[k // a1.shape[1], k % a1.shape[1], 0:1, 0:o_loc]
        for t in others:
            ag_from(a2, a2_send, a2_recv, t).wait_recv()
        spread(a2, half // 8, (0, 2))

    for d in v_first(1) + v_relay(1):
        d.wait_send()

    if packed:
        for d in g_near + [v_near]:
            d.wait_send()

        @pl.when(relays)
        def _():
            for d in g_far + [v_far]:
                d.wait_send()
    else:
        @pl.when(has_next)
        def _():
            g_up.wait_send()
            v_up.wait_send()

        @pl.when(has_prev)
        def _():
            g_down.wait_send()
            v_down.wait_send()

    @pl.when(has_next)
    def _():
        for d in v_first(2) + v_relay(2):
            d.wait_send()

    @pl.when(has_prev)
    def _():
        for d in v_first(0) + v_relay(0):
            d.wait_send()

    for d in ig_out:
        d.wait_send()
    for t in others:
        rs_copy(s1, r1, s1_send, s1_recv, t).wait_send()
        ag_copy(a1, a1_send, a1_recv, t).wait_send()
        rs_copy(s2, r2, s2_send, s2_recv, t).wait_send()
        ag_copy(a2, a2_send, a2_recv, t).wait_send()


def hand_out(feat, ig, kg, bg, feat_o, ig_o, kg_o, bg_o, sems):
    moves = [pltpu.make_async_copy(src, dst, sems.at[k]) for k, (src, dst) in enumerate(
        ((kg, kg_o), (feat, feat_o), (ig, ig_o), (bg, bg_o)))]
    for move in moves:
        move.start()
    for move in moves:
        move.wait()


def on_device(slabs, chans, volume, kernel, bias, out_grad):
    c_loc, _, rows, cols = volume.shape
    c_in, o_loc = kernel.shape[3], kernel.shape[4]
    cells = rows * cols
    packed = o_loc == 32 and c_in == 64 and slabs == 8
    scale = 1.0 / math.sqrt(slabs * cells)
    vmem = pl.BlockSpec(memory_space=pltpu.VMEM)
    parts = slabs if packed else 1
    dma = pltpu.SemaphoreType.DMA
    shapes = (
        jax.ShapeDtypeStruct((o_loc, 1, rows, cols), BF16),
        jax.ShapeDtypeStruct((c_loc, 1, rows, cols), BF16),
        jax.ShapeDtypeStruct((3, 3, 3, o_loc, c_in), F32),
        jax.ShapeDtypeStruct((1, o_loc), F32),
    )
    results = pl.pallas_call(
        functools.partial(body, slabs, chans, packed, scale),
        out_shape=shapes,
        in_specs=[pl.BlockSpec(memory_space=pltpu.HBM)] * 4,
        out_specs=(vmem,) * 4,
        scratch_shapes=[
            pltpu.VMEM(volume.shape, BF16),
            pltpu.VMEM((3, 3, 3, o_loc, c_in), BF16),
            pltpu.VMEM((1, o_loc), F32),
            pltpu.VMEM(out_grad.shape, BF16),
            dma((4,)),
            pltpu.VMEM((max(o_loc, c_loc), rows, cols), F32),
            pltpu.VMEM((3, chans, c_loc, cells), BF16),
            pltpu.VMEM((3, o_loc, cells), BF16),
            pltpu.VMEM((9 * c_in, cells), BF16),
            pltpu.VMEM((9 * o_loc, cells), BF16),
            pltpu.VMEM((3 * c_in, cells), BF16),
            pltpu.VMEM((3 * o_loc, 9 * c_in), BF16),
            pltpu.VMEM((3 * c_in, 9 * o_loc), BF16),
            pltpu.VMEM((chans, c_loc, cells), F32),
            pltpu.VMEM((chans, c_loc, cells), F32),
            pltpu.VMEM((9 * o_loc, 256), F32),
        ] + [pltpu.VMEM((parts, 3, 8, 128), F32)] * 3 + [pltpu.VMEM((parts, 5, 8, 128), F32)] * 3
        + [dma((3, chans)), dma((3, chans)), dma((2,)), dma((2, 2)), dma((3, 2)),
           dma((chans,)), dma((chans,))] + [dma((parts,))] * 8,
        compiler_params=pltpu.CompilerParams(
            collective_id=0, has_side_effects=True, vmem_limit_bytes=64 * 1024 * 1024),
        cost_estimate=pl.CostEstimate(
            flops=3 * 2 * cells * 27 * c_in * o_loc, bytes_accessed=2 * 1024 * 1024,
            transcendentals=0),
    )(volume, jnp.swapaxes(kernel, 3, 4), bias.reshape(1, o_loc), out_grad)
    feature, input_grad, kernel_grad, bias_grad = pl.pallas_call(
        hand_out,
        out_shape=shapes,
        in_specs=[vmem] * 4,
        out_specs=(pl.BlockSpec(memory_space=pl.ANY),) * 4,
        scratch_shapes=[dma((4,))],
        compiler_params=pltpu.CompilerParams(vmem_limit_bytes=64 * 1024 * 1024),
        cost_estimate=pl.CostEstimate(flops=0, bytes_accessed=1024 * 1024, transcendentals=0),
    )(*results)
    bias_grad = bias_grad.reshape(o_loc)
    kernel_grad = jnp.swapaxes(kernel_grad, 3, 4)
    if not packed:
        kernel_grad, bias_grad = lax.psum((kernel_grad, bias_grad), "slab")
        kernel_grad, bias_grad = kernel_grad * scale, bias_grad * scale
    return feature, input_grad, kernel_grad, bias_grad


def solution(mesh):
    specs = (
        P("chan", "slab", None, None),
        P(None, None, None, None, "chan"),
        P("chan"),
        P("chan", "slab", None, None),
    )
    out_specs = (specs[0], specs[0], specs[1], specs[2])
    run = functools.partial(on_device, mesh.shape["slab"], mesh.shape["chan"])
    return jax.shard_map(run, mesh=mesh, in_specs=specs, out_specs=out_specs, check_vma=False)
```

```python
import functools
import math

import jax
import jax.numpy as jnp
from jax import lax
from jax.experimental import pallas as pl
from jax.experimental.pallas import tpu as pltpu
from jax.sharding import PartitionSpec as P

F32 = jnp.float32
BF16 = jnp.bfloat16
MESH = pl.DeviceIdType.MESH


def roll_cols(value, step):
    width = value.shape[-1]
    lane = lax.broadcasted_iota(jnp.int32, value.shape, value.ndim - 1)
    edge = 0 if step > 0 else width - 1
    return jnp.where(lane == edge, 0.0, pltpu.roll(value, step % width, value.ndim - 1))


def body(slabs, chans, packed, scale, vol, ker, bias, og, feat, ig, kg, bg,
         tmp, rv, rg, xv3, xg3, vc, w1, w2, igs, igr, part,
         s1, r1, a1, s2, r2, a2,
         v_send, v_recv, vh_send, g_send, g_recv, ig_send, ig_recv,
         s1_send, s1_recv, a1_send, a1_recv, s2_send, s2_recv, a2_send, a2_recv):
    c_in, o_loc = ker.shape[3], ker.shape[4]
    c_loc, rows, cols = vol.shape[0], vol.shape[2], vol.shape[3]
    cells = rows * cols
    s = lax.axis_index("slab")
    c = lax.axis_index("chan")
    has_prev, has_next = s > 0, s < slabs - 1

    def to_slab(t):
        return {"slab": t}

    def to_chan(t):
        return {"chan": t}

    def other_core(q):
        return q + 1 - 2 * lax.rem(q, 2)

    peers = [lax.rem(c + k, chans) for k in range(1, chans)]
    sib = other_core(c)
    same = [lax.rem(c + 2 * k, chans) for k in range(1, chans // 2)]
    others = [lax.rem(s + k, slabs) for k in range(1, slabs)] if packed else []

    barrier = pltpu.get_barrier_semaphore()
    for p in peers:
        pl.semaphore_signal(barrier, inc=1, device_id=to_chan(p), device_id_type=MESH)
    if packed:
        for t in others:
            pl.semaphore_signal(barrier, inc=1, device_id=to_slab(t), device_id_type=MESH)
    else:
        @pl.when(has_prev)
        def _():
            pl.semaphore_signal(barrier, inc=1, device_id=to_slab(s - 1), device_id_type=MESH)

        @pl.when(has_next)
        def _():
            pl.semaphore_signal(barrier, inc=1, device_id=to_slab(s + 1), device_id_type=MESH)

    tmp[...] = og[:, 0].astype(F32)
    for h in range(rows):
        rg[1, :, h * cols:(h + 1) * cols] = tmp[:, h, :].astype(BF16)
    tmp[:c_loc] = vol[:, 0].astype(F32)
    for h in range(rows):
        rv[1, c, :, h * cols:(h + 1) * cols] = tmp[:c_loc, h, :].astype(BF16)

    if packed:
        pl.semaphore_wait(barrier, chans - 1 + slabs - 1)
    else:
        pl.semaphore_wait(barrier, chans - 1)

        @pl.when(has_prev)
        def _():
            pl.semaphore_wait(barrier, 1)

        @pl.when(has_next)
        def _():
            pl.semaphore_wait(barrier, 1)

    def copy(src, dst, ssem, rsem, dev):
        return pltpu.make_async_remote_copy(
            src_ref=src, dst_ref=dst, send_sem=ssem, recv_sem=rsem,
            device_id=dev, device_id_type=MESH)

    g_up = copy(rg.at[1], rg.at[2], g_send.at[0], g_recv.at[2], to_slab(s + 1))
    g_down = copy(rg.at[1], rg.at[0], g_send.at[1], g_recv.at[0], to_slab(s - 1))
    v_up = copy(rv.at[1, c], rv.at[0, c], vh_send.at[0], v_recv.at[0, c], to_slab(s + 1))
    v_down = copy(rv.at[1, c], rv.at[2, c], vh_send.at[1], v_recv.at[2, c], to_slab(s - 1))

    def v_block(a, q, p, slot):
        return copy(rv.at[a, q], rv.at[a, q], v_send.at[a, slot], v_recv.at[a, q], to_chan(p))

    def v_first(a):
        return [v_block(a, c, p, p) for p in same] + [v_block(a, c, sib, sib)]

    def v_relay(a):
        return [v_block(a, q, sib, other_core(q)) for q in same]

    def v_relay_wait(a):
        for q, d in zip(same, v_relay(a)):
            v_block(a, q, sib, other_core(q)).wait_recv()
            d.start()

    def v_rest_wait(a):
        for q in [sib] + [other_core(q) for q in same]:
            v_block(a, q, sib, q).wait_recv()

    for d in v_first(1):
        d.start()

    @pl.when(has_next)
    def _():
        g_up.start()

    @pl.when(has_prev)
    def _():
        g_down.start()

    order = (0, 2, 1)
    for cc in range(3):
        w2[cc * c_in:(cc + 1) * c_in, :] = jnp.concatenate(
            [ker[a, 2 - j, cc].astype(F32) for a in order for j in range(3)], axis=1
        ).astype(BF16)
    w1t = jnp.concatenate(
        [jnp.concatenate([ker[a, b, cc].astype(F32) for cc in range(3)], axis=1)
         for a in range(3) for b in range(3)], axis=0)
    w1[...] = jnp.transpose(w1t).astype(BF16)

    def windows(dst, base, block):
        n = block.shape[0]
        zero = jnp.zeros((n, cols), BF16)
        at = base * 3 * n
        dst[at:at + n, 0:cols] = zero
        dst[at:at + n, cols:cells] = block[:, 0:cells - cols]
        dst[at + n:at + 2 * n, :] = block
        dst[at + 2 * n:at + 3 * n, 0:cells - cols] = block[:, cols:cells]
        dst[at + 2 * n:at + 3 * n, cells - cols:cells] = zero

    windows(xg3, 2, rg[1])
    nt = (((1,), (1,)), ((), ()))
    bias_part = lax.dot_general(
        jnp.ones((8, cells), BF16), rg[1], nt, preferred_element_type=F32)

    v_relay_wait(1)
    v_rest_wait(1)
    v_own = jnp.concatenate([rv[1, q] for q in range(chans)], axis=0)
    for h in range(rows):
        at = slice(h * cols, (h + 1) * cols)
        block = v_own[:, at]
        wide = block.astype(F32)
        vc[0:c_in, at] = roll_cols(wide, 1).astype(BF16)
        vc[c_in:2 * c_in, at] = block
        vc[2 * c_in:3 * c_in, at] = roll_cols(wide, -1).astype(BF16)

    half = 6 * o_loc
    wide_to = 3 * c_in
    part[half:, 0:wide_to] = lax.dot_general(
        xg3[half:, :], vc[...], nt, preferred_element_type=F32)

    def tiles(start, count):
        found = [part[start + 8 * k:start + 8 * k + 8, 0:128] for k in range(count)]
        for k in range(0, count, 2):
            found.append(jnp.concatenate(
                [part[start + 8 * k:start + 8 * k + 8, 128:192],
                 part[start + 8 * k + 8:start + 8 * k + 16, 128:192]], axis=1))
        return found

    def fill(dst, found):
        per = dst.shape[1]
        found = found + [jnp.zeros((8, 128), F32)] * (per * slabs - len(found))
        for k, tile in enumerate(found):
            dst[k // per, k % per] = tile

    def rs_copy(src, dst, ssem, rsem, t):
        return copy(src.at[t], dst.at[s], ssem.at[t], rsem.at[s], to_slab(t))

    def rs_from(src, dst, ssem, rsem, t):
        return copy(src.at[t], dst.at[t], ssem.at[t], rsem.at[t], to_slab(t))

    def ag_copy(buf, ssem, rsem, t):
        return copy(buf.at[s], buf.at[s], ssem.at[t], rsem.at[s], to_slab(t))

    def ag_from(buf, ssem, rsem, t):
        return copy(buf.at[t], buf.at[t], ssem.at[t], rsem.at[t], to_slab(t))

    def reduce_rows(src, dst, buf, ssem, rsem):
        dst[s] = src[s]
        for t in others:
            rs_from(src, dst, ssem, rsem, t).wait_recv()
        done = dst[0]
        for t in range(1, slabs):
            done = done + dst[t]
        buf[s] = done * scale

    if packed:
        fill(s1, tiles(half, 3 * o_loc // 8)
             + [jnp.concatenate([bias_part, jnp.zeros((8, 128 - o_loc), F32)], axis=1)])
        for t in others:
            rs_copy(s1, r1, s1_send, s1_recv, t).start()

    @pl.when(has_next)
    def _():
        v_up.start()

    @pl.when(has_prev)
    def _():
        v_down.start()

    @pl.when(has_next)
    def _():
        g_down.wait_recv()

    @pl.when(jnp.logical_not(has_next))
    def _():
        rg[0] = jnp.zeros((o_loc, cells), BF16)

    windows(xg3, 0, rg[0])

    @pl.when(has_prev)
    def _():
        g_up.wait_recv()

    @pl.when(jnp.logical_not(has_prev))
    def _():
        rg[2] = jnp.zeros((o_loc, cells), BF16)

    windows(xg3, 1, rg[2])
    part[0:half, 0:wide_to] = lax.dot_general(
        xg3[0:half, :], vc[...], nt, preferred_element_type=F32)
    if packed:
        fill(s2, tiles(0, half // 8))
        for t in others:
            rs_copy(s2, r2, s2_send, s2_recv, t).start()
        reduce_rows(s1, r1, a1, s1_send, s1_recv)
        for t in others:
            ag_copy(a1, a1_send, a1_recv, t).start()

    @pl.when(has_prev)
    def _():
        v_up.wait_recv()
        for d in v_first(0):
            d.start()

    @pl.when(has_next)
    def _():
        v_down.wait_recv()
        for d in v_first(2):
            d.start()

    share = jnp.dot(w2[...], xg3[...], preferred_element_type=F32)
    for h in range(rows):
        at = slice(h * cols, (h + 1) * cols)
        total = (share[c_in:2 * c_in, at] + roll_cols(share[0:c_in, at], -1)
                 + roll_cols(share[2 * c_in:3 * c_in, at], 1))
        for p in range(chans):
            igs[p, :, at] = total[p * c_loc:(p + 1) * c_loc]
    ig_out = [copy(igs.at[p], igr.at[c], ig_send.at[p], ig_recv.at[c], to_chan(p)) for p in peers]
    for d in ig_out:
        d.start()

    @pl.when(has_prev)
    def _():
        v_relay_wait(0)

    @pl.when(has_next)
    def _():
        v_relay_wait(2)

    if packed:
        reduce_rows(s2, r2, a2, s2_send, s2_recv)
        for t in others:
            ag_copy(a2, a2_send, a2_recv, t).start()
    else:
        bg[...] = bias_part[0:1, :]
        for k, a in enumerate(order):
            for j in range(3):
                for cc in range(3):
                    at = (k * 3 + j) * o_loc
                    kg[a, 2 - j, cc] = part[at:at + o_loc, cc * c_in:(cc + 1) * c_in]

    windows(xv3, 1, v_own)
    for a, here in ((0, has_prev), (2, has_next)):
        @pl.when(here)
        def _():
            v_rest_wait(a)

        @pl.when(jnp.logical_not(here))
        def _():
            rv[a] = jnp.zeros((chans, c_loc, cells), BF16)

        windows(xv3, a, jnp.concatenate([rv[a, q] for q in range(chans)], axis=0))
    pre = jnp.dot(w1[...], xv3[...], preferred_element_type=F32)
    bias_col = jnp.transpose(jnp.broadcast_to(bias[...], (cols, o_loc)))
    for h in range(rows):
        at = slice(h * cols, (h + 1) * cols)
        tmp[:, h, :] = (pre[o_loc:2 * o_loc, at] + roll_cols(pre[0:o_loc, at], 1)
                        + roll_cols(pre[2 * o_loc:3 * o_loc, at], -1) + bias_col)
    feat[:, 0] = tmp[...].astype(BF16)

    igr[c] = igs[c]
    for q in peers:
        copy(igs.at[q], igr.at[q], ig_send.at[q], ig_recv.at[q], to_chan(q)).wait_recv()
    for h in range(rows):
        at = slice(h * cols, (h + 1) * cols)
        total = igr[0, :, at]
        for q in range(1, chans):
            total = total + igr[q, :, at]
        tmp[:c_loc, h, :] = total
    ig[:, 0] = tmp[:c_loc].astype(BF16)

    def spread(buf, count, taps):
        per = buf.shape[1]
        for k in range(count):
            a, j, o = taps[k * 8 // (3 * o_loc)], (k * 8 // o_loc) % 3, k * 8 % o_loc
            m = count + k // 2
            low = buf[k // per, k % per]
            kg[a, 2 - j, 0, o:o + 8, :] = low[:, 0:c_in]
            kg[a, 2 - j, 1, o:o + 8, :] = low[:, c_in:2 * c_in]
            at = (k % 2) * c_in
            kg[a, 2 - j, 2, o:o + 8, :] = buf[m // per, m % per, :, at:at + c_in]

    if packed:
        for t in others:
            ag_from(a1, a1_send, a1_recv, t).wait_recv()
        spread(a1, 3 * o_loc // 8, (1,))
        k = (3 * o_loc // 8) * 3 // 2
        bg[...] = a1[k // a1.shape[1], k % a1.shape[1], 0:1, 0:o_loc]
        for t in others:
            ag_from(a2, a2_send, a2_recv, t).wait_recv()
        spread(a2, half // 8, (0, 2))

    for d in v_first(1) + v_relay(1):
        d.wait_send()

    @pl.when(has_next)
    def _():
        g_up.wait_send()
        v_up.wait_send()
        for d in v_first(2) + v_relay(2):
            d.wait_send()

    @pl.when(has_prev)
    def _():
        g_down.wait_send()
        v_down.wait_send()
        for d in v_first(0) + v_relay(0):
            d.wait_send()

    for d in ig_out:
        d.wait_send()
    for t in others:
        rs_copy(s1, r1, s1_send, s1_recv, t).wait_send()
        ag_copy(a1, a1_send, a1_recv, t).wait_send()
        rs_copy(s2, r2, s2_send, s2_recv, t).wait_send()
        ag_copy(a2, a2_send, a2_recv, t).wait_send()


def hand_out(feat, ig, kg, bg, feat_o, ig_o, kg_o, bg_o, sems):
    moves = [pltpu.make_async_copy(src, dst, sems.at[k]) for k, (src, dst) in enumerate(
        ((kg, kg_o), (feat, feat_o), (ig, ig_o), (bg, bg_o)))]
    for move in moves:
        move.start()
    for move in moves:
        move.wait()


def on_device(slabs, chans, volume, kernel, bias, out_grad):
    c_loc, _, rows, cols = volume.shape
    c_in, o_loc = kernel.shape[3], kernel.shape[4]
    cells = rows * cols
    packed = o_loc == 32 and c_in == 64 and slabs == 8
    scale = 1.0 / math.sqrt(slabs * cells)
    vmem = pl.BlockSpec(memory_space=pltpu.VMEM)
    parts = slabs if packed else 1
    dma = pltpu.SemaphoreType.DMA
    shapes = (
        jax.ShapeDtypeStruct((o_loc, 1, rows, cols), BF16),
        jax.ShapeDtypeStruct((c_loc, 1, rows, cols), BF16),
        jax.ShapeDtypeStruct((3, 3, 3, o_loc, c_in), F32),
        jax.ShapeDtypeStruct((1, o_loc), F32),
    )
    results = pl.pallas_call(
        functools.partial(body, slabs, chans, packed, scale),
        out_shape=shapes,
        in_specs=[vmem] * 4,
        out_specs=(vmem,) * 4,
        scratch_shapes=[
            pltpu.VMEM((max(o_loc, c_loc), rows, cols), F32),
            pltpu.VMEM((3, chans, c_loc, cells), BF16),
            pltpu.VMEM((3, o_loc, cells), BF16),
            pltpu.VMEM((9 * c_in, cells), BF16),
            pltpu.VMEM((9 * o_loc, cells), BF16),
            pltpu.VMEM((3 * c_in, cells), BF16),
            pltpu.VMEM((3 * o_loc, 9 * c_in), BF16),
            pltpu.VMEM((3 * c_in, 9 * o_loc), BF16),
            pltpu.VMEM((chans, c_loc, cells), F32),
            pltpu.VMEM((chans, c_loc, cells), F32),
            pltpu.VMEM((9 * o_loc, 256), F32),
        ] + [pltpu.VMEM((parts, 3, 8, 128), F32)] * 3 + [pltpu.VMEM((parts, 5, 8, 128), F32)] * 3
        + [dma((3, chans)), dma((3, chans)), dma((2,)), dma((2,)), dma((3,)),
           dma((chans,)), dma((chans,))] + [dma((parts,))] * 8,
        compiler_params=pltpu.CompilerParams(
            collective_id=0, has_side_effects=True, vmem_limit_bytes=40 * 1024 * 1024),
        cost_estimate=pl.CostEstimate(
            flops=3 * 2 * cells * 27 * c_in * o_loc, bytes_accessed=2 * 1024 * 1024,
            transcendentals=0),
    )(volume, kernel, bias.reshape(1, o_loc), out_grad)
    feature, input_grad, kernel_grad, bias_grad = pl.pallas_call(
        hand_out,
        out_shape=shapes,
        in_specs=[vmem] * 4,
        out_specs=(pl.BlockSpec(memory_space=pl.ANY),) * 4,
        scratch_shapes=[dma((4,))],
        compiler_params=pltpu.CompilerParams(vmem_limit_bytes=8 * 1024 * 1024),
        cost_estimate=pl.CostEstimate(flops=0, bytes_accessed=1024 * 1024, transcendentals=0),
    )(*results)
    bias_grad = bias_grad.reshape(o_loc)
    kernel_grad = jnp.swapaxes(kernel_grad, 3, 4)
    if not packed:
        kernel_grad, bias_grad = lax.psum((kernel_grad, bias_grad), "slab")
        kernel_grad, bias_grad = kernel_grad * scale, bias_grad * scale
    return feature, input_grad, kernel_grad, bias_grad


def solution(mesh):
    specs = (
        P("chan", "slab", None, None),
        P(None, None, None, None, "chan"),
        P("chan"),
        P("chan", "slab", None, None),
    )
    out_specs = (specs[0], specs[0], specs[1], specs[2])
    run = functools.partial(on_device, mesh.shape["slab"], mesh.shape["chan"])
    return jax.shard_map(run, mesh=mesh, in_specs=specs, out_specs=out_specs, check_vma=False)
```
